128 devices in a mesh: dp: 2 (over core), expert: 64 (over z, y, x).
Axes of the slice: x: 4, y: 4, z: 4, core: 2. Of those that a mesh axis runs over, the one named last changes fastest.
Arguments:
- tokens: bfloat16 [32768, 3584], P(('dp', 'expert')), may hold values from -6 to 6
- expert_ids: int32 [32768, 2], P(('dp', 'expert')), may hold values from 0 to 63, all different within a row; in each aligned block of 256 rows (0 to 255, 256 to 511, ...) at most 12 rows name the same one
- gate_weights: float32 [32768, 2], P(('dp', 'expert')), may hold values from 0.2 to 1
- w_in: bfloat16 [64, 3584, 2560], P('expert', None, 'dp'), may hold values from -0.09375 to 0.09375
- w_out: bfloat16 [64, 2560, 3584], P('expert', 'dp'), may hold values from -0.125 to 0.125
Outputs:
- mixed: bfloat16 [32768, 3584], P(('dp', 'expert'))
The draws below stay inside these ranges and needn't reach their ends.
Inputs may be any that keep to these rules, and one draw needn't show every extreme that they name: `expert_ids`: each row names 2 different experts. Among the rows of one device no expert is named more than 12 times, and in every draw some device names some expert exactly 12 times.
All inputs are finite; a program needn't handle non-finite values.
Results may differ from the reference program's by a relative error of at most 0.007.
Values may be sent and summed in bfloat16 or wider, within the bound.
No kernel may reach another device: no remote copies, remote signals or barrier semaphores. Data moves between devices by JAX's collectives and lax.ppermute only.
A program may use at most 192 MiB of HBM per device.

```python
import math
import jax
import jax.numpy as jnp
import numpy as np
from jax import lax

D = 3584
F = 2560
TOP = 2
TOK_DEV = 256
EXPERTS = 64
CAP = 12
TOKENS = 32768
N_DP = 2
N_EXPERT = 64


def shard_levels(rng, dims, cuts, least, largest):
    gain = 1.0
    for position, parts in cuts:
        draws = jax.random.uniform(jax.random.fold_in(jax.random.fold_in(rng, 6), position), (parts,), jnp.float32, least / len(cuts), largest / len(cuts))
        gain = gain * jnp.repeat(jnp.exp(draws), dims[position] // parts).reshape((-1,) + (1,) * (len(dims) - 1 - position))
    return gain


def deal_out(rng, own, number, rows, number_of, top, bound, lean):
    order = jax.random.permutation(rng, number_of)
    heavy_load, ordinary = portions_of(number_of, rows * top, bound, lean, True), portions_of(number_of, rows * top, bound, lean, False)
    places = jnp.arange(number_of)

    def named(sizes, offset_by):
        used = int((sizes > 0).sum())
        fixed = max(1, used // 4)
        moved = fixed + (places - fixed + offset_by * (used - fixed)) % max(1, number_of - fixed)
        return jnp.zeros((number_of,), jnp.int32).at[order[jnp.where(places < fixed, places, moved)]].set(jnp.asarray(sizes, jnp.int32))

    sizes = jnp.where(number % 4 == 0, named(heavy_load, number // 4), named(ordinary, number - number // 4 - 1))
    mixed = jax.random.permutation(jax.random.fold_in(own, 3), number_of)
    giver, receiver = mixed[0:number_of // 2 * 2:2], mixed[1:number_of // 2 * 2:2]
    room = jnp.minimum(sizes[giver] - 1, bound - sizes[receiver]) // 2
    room = jnp.where((giver == order[0]) | (receiver == order[0]) | (sizes[receiver] == 0), 0, jnp.maximum(room, 0))
    moved = jax.random.randint(jax.random.fold_in(own, 4), (number_of // 2,), 0, 1 << 20) % (room + 1)
    sizes = sizes.at[giver].add(-moved).at[receiver].add(moved)
    members = jnp.searchsorted(jnp.cumsum(sizes), jnp.arange(rows * top), side="right").astype(jnp.int32)
    table = members.reshape(top, rows).T
    table = table[jax.random.permutation(jax.random.fold_in(own, 1), rows)]
    offset_by = jax.random.randint(jax.random.fold_in(own, 2), (rows, 1), 0, top)
    return jnp.take_along_axis(table, (jnp.arange(top)[None, :] + offset_by) % top, axis=1)


def portions_of(count, total, limit, lean, full):
    loads = [(1 << 20) // math.isqrt(grade ** lean) + 1 for grade in range(1, count + 1)]
    largest = limit if full else min(limit, max(-(-total // count), total * loads[0] // sum(loads)))
    least = 1 if total - largest >= count - 1 else 0
    holding, surplus = [largest] + [least] * (count - 1), total - largest - least * (count - 1)
    while surplus > 0:
        movable = [i for i in range(1, count) if holding[i] < largest] or [i for i in range(1, count) if holding[i] < limit]
        pool, left = sum([loads[i] for i in movable]), surplus
        for i in movable:
            extra = min(limit - holding[i], max(1, left * loads[i] // pool), surplus)
            holding[i] = holding[i] + extra
            surplus = surplus - extra
    return np.array(holding)


def scatter_about(stream_key, shape, deviation, bound, shards=(), kind=jnp.bfloat16):
    entries = deviation * jax.random.normal(stream_key, shape, jnp.float32)
    if shards:
        entries = entries * shard_levels(stream_key, shape, shards, -0.22, 0.18)
    return jnp.clip(entries, -bound, bound).astype(kind)


def setup_inputs(seed: int = 0) -> dict:
    key_list = jax.random.split(jax.random.key(seed), 6)
    tokens = scatter_about(key_list[0], (TOKENS, D), 1.0, 6.0, ((0, 128),))
    expert_ids_keys = jax.random.split(jax.random.fold_in(key_list[1], 1), TOKENS // TOK_DEV)
    expert_ids_turns = jax.random.permutation(jax.random.fold_in(key_list[1], 3), TOKENS // TOK_DEV)
    expert_ids = jax.vmap(lambda own, number: deal_out(jax.random.fold_in(key_list[1], 2), own, number, TOK_DEV, EXPERTS, TOP, CAP, 2))(expert_ids_keys, expert_ids_turns).reshape((TOKENS, TOP))
    gate_weights = jnp.clip(0.2 + 0.8 * jax.random.uniform(key_list[2], (TOKENS, TOP), jnp.float32) ** shard_levels(key_list[2], (TOKENS, TOP), ((0, 128),), -0.2, 0.2), 0.2, 1.0)
    w_in = scatter_about(key_list[3], (EXPERTS, D, F), D ** -0.5, 0.09375, ((0, 64), (2, 2)))
    w_out = scatter_about(key_list[4], (EXPERTS, F, D), F ** -0.5, 0.125, ((0, 64), (1, 2)))
    return {"tokens": tokens, "expert_ids": expert_ids, "gate_weights": gate_weights, "w_in": w_in, "w_out": w_out}


def reference(tokens, expert_ids, gate_weights, w_in, w_out):
    bound_all = N_DP * N_EXPERT * CAP
    flat_ids = expert_ids.reshape(-1)
    flat_gates = gate_weights.reshape(-1)
    block_width = F // N_DP

    def one_expert(running, expert):
        matches = flat_ids == expert
        chosen = jnp.nonzero(matches, size=bound_all, fill_value=0)[0].astype(jnp.int32)
        live = (jnp.arange(bound_all, dtype=jnp.int32) < jnp.sum(matches.astype(jnp.int32))).astype(jnp.float32)
        token_index = chosen // TOP
        inputs = tokens[token_index]
        weight_in = lax.dynamic_index_in_dim(w_in, expert, 0, keepdims=False)
        weight_out = lax.dynamic_index_in_dim(w_out, expert, 0, keepdims=False)
        hidden = jax.nn.silu(jnp.dot(inputs, weight_in, preferred_element_type=jnp.float32)).astype(jnp.bfloat16)
        total = jnp.zeros((bound_all, D), jnp.float32)
        for block in range(N_DP):
            part_sum = jnp.dot(hidden[:, block * block_width:(block + 1) * block_width], weight_out[block * block_width:(block + 1) * block_width], preferred_element_type=jnp.float32)
            total = total + part_sum.astype(jnp.bfloat16).astype(jnp.float32)
        outputs = total.astype(jnp.bfloat16)
        scaled = outputs.astype(jnp.float32) * (flat_gates[chosen] * live)[:, None]
        return running.at[token_index].add(scaled), None

    start = jnp.zeros((TOKENS, D), jnp.float32)
    mixed, unused = lax.scan(one_expert, start, jnp.arange(EXPERTS, dtype=jnp.int32))
    return (tokens.astype(jnp.float32) + mixed).astype(jnp.bfloat16)
```

```python
import functools

import jax
import jax.numpy as jnp
from jax import lax
from jax.experimental import pallas as pl
from jax.experimental.pallas import tpu as pltpu
from jax.sharding import PartitionSpec as P

PACK = 8
EXTRA = 4
BF16 = jnp.bfloat16
F32 = jnp.float32


def iota(shape, dim):
    return lax.broadcasted_iota(jnp.int32, shape, dim)


def dot(a, b):
    return jnp.dot(a, b, preferred_element_type=F32)


def dot_t(a, b):
    return lax.dot_general(a, b, (((0,), (0,)), ((), ())), preferred_element_type=F32)


def prep_kernel(ids_ref, tok_ref, place_ref, out_ref, *, peers):
    tokens = tok_ref.shape[0]
    width = tok_ref.shape[1]
    half = width // 2
    rows = peers * PACK
    before = (iota((tokens, tokens), 0) < iota((tokens, tokens), 1)).astype(BF16)
    experts = iota((peers, tokens), 0)
    first = experts == ids_ref[0:1, :]
    second = experts == ids_ref[1:2, :]
    first_f, second_f = first.astype(F32), second.astype(F32)
    rank0 = jnp.sum(dot(first.astype(BF16), before) * first_f, 0, keepdims=True)
    count0 = jnp.sum(first_f, 1, keepdims=True)
    rank1 = jnp.sum((dot(second.astype(BF16), before) + count0) * second_f, 0, keepdims=True)
    rank = jnp.concatenate([rank0, rank1], 0).astype(jnp.int32)
    base = ids_ref[...] * PACK + rank
    whole = jnp.where(rank < PACK, base, -rows)
    split = jnp.where(rank < PACK, -rows, base - PACK)
    place_ref[0:2, :] = whole
    place_ref[2:4, :] = split
    row = iota((rows, tokens), 0)
    pick = ((row == whole[0:1, :]) | (row == whole[1:2, :])).astype(BF16)
    left = ((row == split[0:1, :]) | (row == split[1:2, :])).astype(BF16)
    right = ((row == split[0:1, :] + EXTRA) | (row == split[1:2, :] + EXTRA)).astype(BF16)
    step = width // 7
    for c in range(0, width, step):
        out_ref[:, c : c + step] = dot(pick, tok_ref[:, c : c + step]).astype(BF16)
    step = half // 7
    for c in range(0, half, step):
        part = dot(left, tok_ref[:, c : c + step])
        part = part + dot(right, tok_ref[:, half + c : half + c + step])
        out_ref[:, width + c : width + c + step] = part.astype(BF16)


def prep(ids, tokens, peers):
    count, width = tokens.shape
    return pl.pallas_call(
        functools.partial(prep_kernel, peers=peers),
        out_shape=(
            jax.ShapeDtypeStruct((4, count), jnp.int32),
            jax.ShapeDtypeStruct((peers * PACK, width + width // 2), BF16),
        ),
        compiler_params=pltpu.CompilerParams(vmem_limit_bytes=40 * 2**20),
        name="dispatch_rows",
    )(ids, tokens)


def combine_kernel(place_ref, gate_ref, tok_ref, back_ref, out_ref):
    tokens, width = tok_ref.shape
    half = width // 2
    rows = back_ref.shape[0]
    row = iota((rows, tokens), 0)
    g0, g1 = gate_ref[0:1, :], gate_ref[1:2, :]

    def weights(p0, p1):
        w = jnp.where(row == p0, g0, 0.0) + jnp.where(row == p1, g1, 0.0)
        high = w.astype(BF16)
        return high, (w - high.astype(F32)).astype(BF16)

    whole = weights(place_ref[0:1, :], place_ref[1:2, :])
    left = weights(place_ref[2:3, :], place_ref[3:4, :])
    right = weights(place_ref[2:3, :] + EXTRA, place_ref[3:4, :] + EXTRA)
    step = half // 7
    for side, extra in ((0, left), (1, right)):
        for c in range(0, half, step):
            at = side * half + c
            total = tok_ref[:, at : at + step].astype(F32)
            for w in whole:
                total = total + dot_t(w, back_ref[:, at : at + step])
            for w in extra:
                total = total + dot_t(w, back_ref[:, width + c : width + c + step])
            out_ref[:, at : at + step] = total.astype(BF16)


def combine(place, gates, tokens, back):
    return pl.pallas_call(
        combine_kernel,
        out_shape=jax.ShapeDtypeStruct(tokens.shape, BF16),
        compiler_params=pltpu.CompilerParams(vmem_limit_bytes=40 * 2**20),
        name="weighted_rows",
    )(place, gates, tokens, back)


def silu(v):
    return v / (1.0 + jnp.exp(-v))


def ffn_kernel(x_ref, win_ref, wout_ref, o_ref, x2, h, y2, *, n1, n2, fw, dw, mc):
    step = pl.program_id(0)
    rows = x_ref.shape[0]
    width = x2.shape[1]
    half = width // 2
    more = x2.shape[0]

    @pl.when(step == 0)
    def _():
        source = iota((more, rows), 0) // EXTRA * PACK + iota((more, rows), 0) % EXTRA
        column = iota((more, rows), 1)
        packed = x_ref[:, width:]
        x2[:, :half] = dot((source == column).astype(BF16), packed).astype(BF16)
        x2[:, half:] = dot((source + EXTRA == column).astype(BF16), packed).astype(BF16)

    @pl.when(step < n1)
    def _():
        c = pl.ds(pl.multiple_of(step * fw, fw), fw)
        for m in range(0, rows, mc):
            h[m : m + mc, c] = silu(dot(x_ref[m : m + mc, :width], win_ref[...])).astype(BF16)
        for m in range(0, more, mc):
            h[rows + m : rows + m + mc, c] = silu(dot(x2[m : m + mc, :], win_ref[...])).astype(BF16)

    @pl.when(step >= n1)
    def _():
        c = pl.ds(pl.multiple_of((step - n1) * dw, dw), dw)
        for m in range(0, rows, mc):
            o_ref[m : m + mc, c] = dot(h[m : m + mc, :], wout_ref[...]).astype(BF16)
        for m in range(0, more, mc):
            y2[m : m + mc, c] = dot(h[rows + m : rows + m + mc, :], wout_ref[...]).astype(BF16)

    @pl.when(step == n1 + n2 - 1)
    def _():
        row = iota((rows, more), 0)
        source = iota((rows, more), 1) // EXTRA * PACK + iota((rows, more), 1) % EXTRA
        packed = dot((row == source).astype(BF16), y2[:, :half])
        packed = packed + dot((row == source + EXTRA).astype(BF16), y2[:, half:])
        o_ref[:, width:] = packed.astype(BF16)


def ffn(x, w_in, w_out, fw=512, dw=512, mc=256):
    width, hidden = w_in.shape
    rows = x.shape[0]
    more = rows // PACK * EXTRA
    n1, n2 = hidden // fw, width // dw
    return pl.pallas_call(
        functools.partial(ffn_kernel, n1=n1, n2=n2, fw=fw, dw=dw, mc=mc),
        out_shape=jax.ShapeDtypeStruct(x.shape, BF16),
        grid=(n1 + n2,),
        in_specs=[
            pl.BlockSpec(x.shape, lambda i: (0, 0), pipeline_mode=pl.Buffered(1)),
            pl.BlockSpec((width, fw), lambda i: (0, jnp.minimum(i, n1 - 1))),
            pl.BlockSpec((hidden, dw), lambda i: (0, jnp.maximum(i - n1, 0))),
        ],
        out_specs=pl.BlockSpec(x.shape, lambda i: (0, 0), pipeline_mode=pl.Buffered(1)),
        scratch_shapes=[
            pltpu.VMEM((more, width), BF16),
            pltpu.VMEM((rows + more, hidden), BF16),
            pltpu.VMEM((more, width), BF16),
        ],
        compiler_params=pltpu.CompilerParams(vmem_limit_bytes=50 * 2**20),
        cost_estimate=pl.CostEstimate(
            flops=4 * (rows + more) * width * hidden,
            bytes_accessed=4 * width * hidden + 4 * x.size,
            transcendentals=(rows + more) * hidden,
        ),
        name="expert_layer",
    )(x, w_in, w_out)


def swap(x, peers):
    chunks = x.reshape(peers, x.shape[0] // peers, x.shape[1])
    return lax.all_to_all(chunks, "expert", split_axis=0, concat_axis=0, tiled=True).reshape(x.shape)


def per_device(tokens, expert_ids, gate_weights, w_in, w_out):
    peers = lax.axis_size("expert")
    full_in = lax.all_gather(w_in, "dp", axis=2, tiled=True)[0]
    full_out = lax.all_gather(w_out, "dp", axis=1, tiled=True)[0]
    place, sent = prep(expert_ids.T, tokens, peers)
    arrived = swap(sent, peers)
    outgoing = ffn(arrived, full_in, full_out)
    returned = swap(outgoing, peers)
    return combine(place, gate_weights.T, tokens, returned)


def solution(mesh):
    placed = (
        P(("dp", "expert"), None),
        P(("dp", "expert"), None),
        P(("dp", "expert"), None),
        P("expert", None, "dp"),
        P("expert", "dp", None),
    )
    return jax.shard_map(
        per_device, mesh=mesh, in_specs=placed, out_specs=P(("dp", "expert"), None), check_vma=False
    )
```

```python
import functools

import jax
import jax.numpy as jnp
from jax import lax
from jax.experimental import pallas as pl
from jax.experimental.pallas import tpu as pltpu
from jax.sharding import PartitionSpec as P

PACK = 8
EXTRA = 4
BF16 = jnp.bfloat16
F32 = jnp.float32


def iota(shape, dim):
    return lax.broadcasted_iota(jnp.int32, shape, dim)


def dot(a, b):
    return jnp.dot(a, b, preferred_element_type=F32)


def dot_t(a, b):
    return lax.dot_general(a, b, (((0,), (0,)), ((), ())), preferred_element_type=F32)


def prep_kernel(ids_ref, tok_ref, place_ref, out_ref, *, peers):
    tokens = tok_ref.shape[0]
    width = tok_ref.shape[1]
    half = width // 2
    rows = peers * PACK
    before = (iota((tokens, tokens), 0) < iota((tokens, tokens), 1)).astype(BF16)
    experts = iota((peers, tokens), 0)
    first = experts == ids_ref[0:1, :]
    second = experts == ids_ref[1:2, :]
    first_f, second_f = first.astype(F32), second.astype(F32)
    rank0 = jnp.sum(dot(first.astype(BF16), before) * first_f, 0, keepdims=True)
    count0 = jnp.sum(first_f, 1, keepdims=True)
    rank1 = jnp.sum((dot(second.astype(BF16), before) + count0) * second_f, 0, keepdims=True)
    rank = jnp.concatenate([rank0, rank1], 0).astype(jnp.int32)
    base = ids_ref[...] * PACK + rank
    whole = jnp.where(rank < PACK, base, -rows)
    split = jnp.where(rank < PACK, -rows, base - PACK)
    place_ref[0:2, :] = whole
    place_ref[2:4, :] = split
    row = iota((rows, tokens), 0)
    pick = ((row == whole[0:1, :]) | (row == whole[1:2, :])).astype(BF16)
    left = ((row == split[0:1, :]) | (row == split[1:2, :])).astype(BF16)
    right = ((row == split[0:1, :] + EXTRA) | (row == split[1:2, :] + EXTRA)).astype(BF16)
    step = width // 7
    for c in range(0, width, step):
        out_ref[:, c : c + step] = dot(pick, tok_ref[:, c : c + step]).astype(BF16)
    step = half // 7
    for c in range(0, half, step):
        part = dot(left, tok_ref[:, c : c + step])
        part = part + dot(right, tok_ref[:, half + c : half + c + step])
        out_ref[:, width + c : width + c + step] = part.astype(BF16)


def prep(ids, tokens, peers):
    count, width = tokens.shape
    return pl.pallas_call(
        functools.partial(prep_kernel, peers=peers),
        out_shape=(
            jax.ShapeDtypeStruct((4, count), jnp.int32),
            jax.ShapeDtypeStruct((peers * PACK, width + width // 2), BF16),
        ),
        compiler_params=pltpu.CompilerParams(vmem_limit_bytes=40 * 2**20),
        name="dispatch_rows",
    )(ids, tokens)


def combine_kernel(place_ref, gate_ref, tok_ref, back_ref, out_ref):
    tokens, width = tok_ref.shape
    half = width // 2
    rows = back_ref.shape[0]
    row = iota((rows, tokens), 0)
    g0, g1 = gate_ref[0:1, :], gate_ref[1:2, :]

    def weights(p0, p1):
        return (jnp.where(row == p0, g0, 0.0) + jnp.where(row == p1, g1, 0.0)).astype(BF16)

    whole = weights(place_ref[0:1, :], place_ref[1:2, :])
    left = weights(place_ref[2:3, :], place_ref[3:4, :])
    right = weights(place_ref[2:3, :] + EXTRA, place_ref[3:4, :] + EXTRA)
    step = half // 7
    for side, extra in ((0, left), (1, right)):
        for c in range(0, half, step):
            at = side * half + c
            total = tok_ref[:, at : at + step].astype(F32)
            total = total + dot_t(whole, back_ref[:, at : at + step])
            total = total + dot_t(extra, back_ref[:, width + c : width + c + step])
            out_ref[:, at : at + step] = total.astype(BF16)


def combine(place, gates, tokens, back):
    return pl.pallas_call(
        combine_kernel,
        out_shape=jax.ShapeDtypeStruct(tokens.shape, BF16),
        compiler_params=pltpu.CompilerParams(vmem_limit_bytes=40 * 2**20),
        name="weighted_rows",
    )(place, gates, tokens, back)


def silu(v):
    return 0.5 * v * (1.0 + jnp.tanh(0.5 * v))


def expert_kernel(
    x_hbm, ia, ib, oa, ob, y_hbm, pack, x, wi, wo, h, y, y2, sx, si, so, sy, *, fw, dw, ahead
):
    rows, packed_width = pack.shape
    width = x.shape[1]
    more = x.shape[0] - rows
    hid = ia.shape[1]
    n1, n2 = hid // fw, width // dw

    def part(at, size):
        return pl.ds(pl.multiple_of(at * size, size), size)

    def for_tile(t, act):
        @pl.when(t < n1)
        def _():
            act(pltpu.make_async_copy(ia.at[:, part(t, fw)], wi.at[t], si.at[t]))

        @pl.when((t >= n1) & (t < 2 * n1))
        def _():
            act(pltpu.make_async_copy(ib.at[:, part(t - n1, fw)], wi.at[t], si.at[t]))

        @pl.when((t >= 2 * n1) & (t < 2 * n1 + n2))
        def _():
            j = t - 2 * n1
            for k, src in ((0, oa), (1, ob)):
                dst = wo.at[j, pl.ds(k * hid, hid)]
                act(pltpu.make_async_copy(src.at[:, part(j, dw)], dst, so.at[k, j]))

    def start(t):
        for_tile(t, lambda copy: copy.start())

    def wait(t):
        for_tile(t, lambda copy: copy.wait())

    fetch_pack = pltpu.make_async_copy(x_hbm.at[:, pl.ds(width, packed_width)], pack, sx.at[0])
    fetch = pltpu.make_async_copy(x_hbm.at[:, pl.ds(0, width)], x.at[pl.ds(0, rows)], sx.at[1])
    fetch_pack.start()
    fetch.start()

    @pl.loop(0, ahead)
    def _(t):
        start(t)

    fetch_pack.wait()
    source = iota((more, rows), 0) // EXTRA * PACK + iota((more, rows), 0) % EXTRA
    column = iota((more, rows), 1)
    x[rows:, :packed_width] = dot((source == column).astype(BF16), pack[...]).astype(BF16)
    x[rows:, packed_width:] = dot((source + EXTRA == column).astype(BF16), pack[...]).astype(BF16)
    fetch.wait()

    @pl.loop(0, 2 * n1)
    def _(t):
        start(t + ahead)
        wait(t)
        h[:, part(t, fw)] = silu(dot(x[...], wi[t])).astype(BF16)

    def store(j):
        return pltpu.make_async_copy(y.at[j], y_hbm.at[:, part(j, dw)], sy.at[j])

    @pl.loop(0, n2)
    def _(j):
        start(2 * n1 + j + ahead)
        wait(2 * n1 + j)
        y[j] = dot(h[:rows, :], wo[j]).astype(BF16)
        store(j).start()
        y2[:, part(j, dw)] = dot(h[rows:, :], wo[j]).astype(BF16)

    row = iota((rows, more), 0)
    origin = iota((rows, more), 1) // EXTRA * PACK + iota((rows, more), 1) % EXTRA
    left, right = (row == origin).astype(BF16), (row == origin + EXTRA).astype(BF16)
    pack[...] = (dot(left, y2[:, :packed_width]) + dot(right, y2[:, packed_width:])).astype(BF16)
    store_pack = pltpu.make_async_copy(pack, y_hbm.at[:, pl.ds(width, packed_width)], sx.at[0])
    store_pack.start()

    @pl.loop(0, n2)
    def _(j):
        store(j).wait()

    store_pack.wait()


def expert(x, own_in, other_in, own_out, other_out, fw=256, dw=512, ahead=3):
    width, hid = own_in.shape
    rows = x.shape[0]
    more = rows // PACK * EXTRA
    n1, n2 = hid // fw, width // dw
    anywhere = pl.BlockSpec(memory_space=pl.ANY)
    return pl.pallas_call(
        functools.partial(expert_kernel, fw=fw, dw=dw, ahead=ahead),
        out_shape=jax.ShapeDtypeStruct(x.shape, BF16),
        in_specs=[anywhere] * 5,
        out_specs=anywhere,
        scratch_shapes=[
            pltpu.VMEM((rows, width // 2), BF16),
            pltpu.VMEM((rows + more, width), BF16),
            pltpu.VMEM((2 * n1, width, fw), BF16),
            pltpu.VMEM((n2, 2 * hid, dw), BF16),
            pltpu.VMEM((rows + more, 2 * hid), BF16),
            pltpu.VMEM((n2, rows, dw), BF16),
            pltpu.VMEM((more, width), BF16),
            pltpu.SemaphoreType.DMA((2,)),
            pltpu.SemaphoreType.DMA((2 * n1,)),
            pltpu.SemaphoreType.DMA((2, n2)),
            pltpu.SemaphoreType.DMA((n2,)),
        ],
        compiler_params=pltpu.CompilerParams(vmem_limit_bytes=60 * 2**20),
        cost_estimate=pl.CostEstimate(
            flops=8 * (rows + more) * width * hid,
            bytes_accessed=8 * width * hid + 4 * x.size,
            transcendentals=2 * (rows + more) * hid,
        ),
        name="expert_layer",
    )(x, own_in, other_in, own_out, other_out)


def swap(x, peers):
    chunks = x.reshape(peers, x.shape[0] // peers, x.shape[1])
    return lax.all_to_all(chunks, "expert", split_axis=0, concat_axis=0, tiled=True).reshape(x.shape)


def per_device(tokens, expert_ids, gate_weights, w_in, w_out):
    peers = lax.axis_size("expert")
    cores = lax.axis_size("dp")
    turn = [(i, (i + 1) % cores) for i in range(cores)]
    other_in = lax.ppermute(w_in, "dp", turn)
    other_out = lax.ppermute(w_out, "dp", turn)
    first = lax.axis_index("dp") == 0

    def dispatch(ids, tokens):
        place, sent = prep(ids, tokens, peers)
        return place, swap(sent, peers)

    def blank(ids, tokens):
        shapes = jax.eval_shape(dispatch, ids, tokens)
        return tuple(jnp.zeros(s.shape, s.dtype) for s in shapes)

    routed = lax.cond(first, dispatch, blank, expert_ids.T, tokens)
    routed, other_in, other_out = lax.optimization_barrier((routed, other_in, other_out))
    place, arrived = lax.cond(
        first, lambda routed, ids, tokens: routed, lambda routed, ids, tokens: dispatch(ids, tokens),
        routed, expert_ids.T, tokens,
    )
    outgoing = expert(arrived, w_in[0], other_in[0], w_out[0], other_out[0])
    returned = swap(outgoing, peers)
    return combine(place, gate_weights.T, tokens, returned)


def solution(mesh):
    placed = (
        P(("dp", "expert"), None),
        P(("dp", "expert"), None),
        P(("dp", "expert"), None),
        P("expert", None, "dp"),
        P("expert", "dp", None),
    )
    return jax.shard_map(
        per_device, mesh=mesh, in_specs=placed, out_specs=P(("dp", "expert"), None), check_vma=False
    )
```

```python
import functools

import jax
import jax.numpy as jnp
from jax import lax
from jax.experimental import pallas as pl
from jax.experimental.pallas import tpu as pltpu
from jax.sharding import PartitionSpec as P

PACK = 8
EXTRA = 4
BF16 = jnp.bfloat16
F32 = jnp.float32


def iota(shape, dim):
    return lax.broadcasted_iota(jnp.int32, shape, dim)


def dot(a, b):
    return jnp.dot(a, b, preferred_element_type=F32)


def dot_t(a, b):
    return lax.dot_general(a, b, (((0,), (0,)), ((), ())), preferred_element_type=F32)


def prep_kernel(ids_ref, tok_ref, place_ref, out_ref, *pack_refs, peers):
    tokens = tok_ref.shape[0]
    width = tok_ref.shape[1]
    half = width // 2
    rows = peers * PACK
    before = (iota((tokens, tokens), 0) < iota((tokens, tokens), 1)).astype(BF16)
    experts = iota((peers, tokens), 0)
    first = experts == ids_ref[0:1, :]
    second = experts == ids_ref[1:2, :]
    first_f, second_f = first.astype(F32), second.astype(F32)
    rank0 = jnp.sum(dot(first.astype(BF16), before) * first_f, 0, keepdims=True)
    count0 = jnp.sum(first_f, 1, keepdims=True)
    rank1 = jnp.sum((dot(second.astype(BF16), before) + count0) * second_f, 0, keepdims=True)
    rank = jnp.concatenate([rank0, rank1], 0).astype(jnp.int32)
    base = ids_ref[...] * PACK + rank
    whole = jnp.where(rank < PACK, base, -rows)
    split = jnp.where(rank < PACK, -rows, base - PACK)
    place_ref[0:2, :] = whole
    place_ref[2:4, :] = split
    row = iota((rows, tokens), 0)
    pick = ((row == whole[0:1, :]) | (row == whole[1:2, :])).astype(BF16)
    left = ((row == split[0:1, :]) | (row == split[1:2, :])).astype(BF16)
    right = ((row == split[0:1, :] + EXTRA) | (row == split[1:2, :] + EXTRA)).astype(BF16)
    step = width // 7
    for c in range(0, width, step):
        out_ref[:, c : c + step] = dot(pick, tok_ref[:, c : c + step]).astype(BF16)
    step = half // 7
    for c in range(0, half, step):
        part = dot(left, tok_ref[:, c : c + step])
        part = part + dot(right, tok_ref[:, half + c : half + c + step])
        if pack_refs:
            pack_refs[0][:, c : c + step] = part.astype(BF16)
        else:
            out_ref[:, width + c : width + c + step] = part.astype(BF16)


def prep(ids, tokens, peers, apart):
    count, width = tokens.shape
    pack = (jax.ShapeDtypeStruct((peers * PACK, width // 2), BF16),) if apart else ()
    sent = width if apart else width + width // 2
    return pl.pallas_call(
        functools.partial(prep_kernel, peers=peers),
        out_shape=(
            jax.ShapeDtypeStruct((4, count), jnp.int32),
            jax.ShapeDtypeStruct((peers * PACK, sent), BF16),
        )
        + pack,
        compiler_params=pltpu.CompilerParams(vmem_limit_bytes=40 * 2**20),
        name="dispatch_rows",
    )(ids, tokens)


def combine_kernel(place_ref, gate_ref, tok_ref, back_ref, pack_ref, out_ref):
    tokens, width = tok_ref.shape
    half = width // 2
    rows = back_ref.shape[0]
    row = iota((rows, tokens), 0)
    g0, g1 = gate_ref[0:1, :], gate_ref[1:2, :]

    def weights(p0, p1):
        return (jnp.where(row == p0, g0, 0.0) + jnp.where(row == p1, g1, 0.0)).astype(BF16)

    whole = weights(place_ref[0:1, :], place_ref[1:2, :])
    left = weights(place_ref[2:3, :], place_ref[3:4, :])
    right = weights(place_ref[2:3, :] + EXTRA, place_ref[3:4, :] + EXTRA)
    step = half // 7
    for side, extra in ((0, left), (1, right)):
        for c in range(0, half, step):
            at = side * half + c
            total = tok_ref[:, at : at + step].astype(F32)
            total = total + dot_t(whole, back_ref[:, at : at + step])
            total = total + dot_t(extra, pack_ref[:, c : c + step])
            out_ref[:, at : at + step] = total.astype(BF16)


def combine(place, gates, tokens, whole, pack, room):
    count, width = tokens.shape
    rows = whole.shape[0]

    def block(shape, at=0):
        return pl.BlockSpec(shape, lambda i: (0, at))

    return pl.pallas_call(
        combine_kernel,
        out_shape=jax.ShapeDtypeStruct(tokens.shape, BF16),
        grid=(1,),
        in_specs=[
            block(place.shape),
            block(gates.shape),
            block(tokens.shape),
            block((rows, width)),
            block((rows, width // 2), 2 if pack.shape[1] > width // 2 else 0),
        ],
        out_specs=block(tokens.shape),
        compiler_params=pltpu.CompilerParams(vmem_limit_bytes=room * 2**20),
        name="weighted_rows",
    )(place, gates, tokens, whole, pack)


def gate_weights_of(row, place, gate):
    w = jnp.where(row == place[0:1, :], gate[0:1, :], 0.0)
    return (w + jnp.where(row == place[1:2, :], gate[1:2, :], 0.0)).astype(BF16)


def sum_whole_kernel(place_ref, gate_ref, tok_ref, back_ref, out_ref):
    tokens, width = tok_ref.shape
    row = iota((back_ref.shape[0], tokens), 0)
    whole = gate_weights_of(row, place_ref[0:2, :], gate_ref[...])
    step = width // 14
    for c in range(0, width, step):
        out_ref[:, c : c + step] = tok_ref[:, c : c + step].astype(F32) + dot_t(whole, back_ref[:, c : c + step])


def sum_packed_kernel(place_ref, gate_ref, part_ref, pack_ref, out_ref):
    tokens, width = part_ref.shape
    half = width // 2
    row = iota((pack_ref.shape[0], tokens), 0)
    step = half // 7
    for side in range(2):
        extra = gate_weights_of(row, place_ref[2:4, :] + EXTRA * side, gate_ref[...])
        for c in range(0, half, step):
            at = side * half + c
            total = part_ref[:, at : at + step] + dot_t(extra, pack_ref[:, c : c + step])
            out_ref[:, at : at + step] = total.astype(BF16)


def add_rows(kernel, place, gates, base, back, out_type, name):
    count, width = base.shape
    rows = back.shape[0]

    def block(shape):
        return pl.BlockSpec(shape, lambda i: (0, 0))

    return pl.pallas_call(
        kernel,
        out_shape=jax.ShapeDtypeStruct(base.shape, out_type),
        grid=(1,),
        in_specs=[
            block(place.shape),
            block(gates.shape),
            block(base.shape),
            block((rows, min(width, back.shape[1]))),
        ],
        out_specs=block(base.shape),
        compiler_params=pltpu.CompilerParams(vmem_limit_bytes=32 * 2**20),
        cost_estimate=pl.CostEstimate(
            flops=2 * rows * base.size, bytes_accessed=12 * base.size, transcendentals=0
        ),
        name=name,
    )(place, gates, base, back)


def silu(v):
    return 0.5 * v * (1.0 + jnp.tanh(0.5 * v))


def expert_kernel(
    x_hbm, ia, ib, oa, ob, *refs, whole, packed, fw, dw, ahead
):
    y_hbm, pack, x, wi, wo, h, y, y2, sx, si, so, sy = refs[-12:]
    wire = x_hbm.shape[0]
    width = x.shape[1]
    half = width // 2
    rows = wire if whole else 0
    more = x.shape[0] - rows
    hid = ia.shape[1]
    n1, n2 = hid // fw, width // dw
    beside = refs[0] if len(refs) > 12 else None

    def part(at, size):
        return pl.ds(pl.multiple_of(at * size, size), size)

    def for_tile(t, act):
        @pl.when(t < n1)
        def _():
            act(pltpu.make_async_copy(ia.at[:, part(t, fw)], wi.at[t], si.at[t]))

        @pl.when((t >= n1) & (t < 2 * n1))
        def _():
            act(pltpu.make_async_copy(ib.at[:, part(t - n1, fw)], wi.at[t], si.at[t]))

        @pl.when((t >= 2 * n1) & (t < 2 * n1 + n2))
        def _():
            j = t - 2 * n1
            for k, src in ((0, oa), (1, ob)):
                dst = wo.at[j, pl.ds(k * hid, hid)]
                act(pltpu.make_async_copy(src.at[:, part(j, dw)], dst, so.at[k, j]))

    def start(t):
        for_tile(t, lambda copy: copy.start())

    def wait(t):
        for_tile(t, lambda copy: copy.wait())

    if packed:
        columns = pl.ds(width, half)
        fetch_pack = pltpu.make_async_copy(x_hbm.at[:, columns], pack, sx.at[0])
        fetch_pack.start()
    if whole:
        columns = pl.ds(0, width)
        fetch = pltpu.make_async_copy(x_hbm.at[:, columns], x.at[pl.ds(0, rows)], sx.at[1])
        fetch.start()

    @pl.loop(0, ahead)
    def _(t):
        start(t)

    if beside is not None:
        bring = pltpu.make_async_copy(beside, pack, sx.at[0])
        bring.start()
    if packed:
        fetch_pack.wait()
        source = iota((more, wire), 0) // EXTRA * PACK + iota((more, wire), 0) % EXTRA
        column = iota((more, wire), 1)
        x[rows:, :half] = dot((source == column).astype(BF16), pack[...]).astype(BF16)
        x[rows:, half:] = dot((source + EXTRA == column).astype(BF16), pack[...]).astype(BF16)
    if whole:
        fetch.wait()

    @pl.loop(0, 2 * n1)
    def _(t):
        start(t + ahead)
        wait(t)
        h[:, part(t, fw)] = silu(dot(x[...], wi[t])).astype(BF16)

    if beside is not None:
        bring.wait()
        leave = pltpu.make_async_copy(pack, y_hbm.at[:, pl.ds(width, half)], sx.at[0])
        leave.start()

    def store(j):
        return pltpu.make_async_copy(y.at[j], y_hbm.at[:, part(j, dw)], sy.at[j])

    @pl.loop(0, n2)
    def _(j):
        start(2 * n1 + j + ahead)
        wait(2 * n1 + j)
        if whole:
            y[j] = dot(h[:rows, :], wo[j]).astype(BF16)
            store(j).start()
        if packed:
            y2[:, part(j, dw)] = dot(h[rows:, :], wo[j]).astype(BF16)

    if packed:
        row = iota((wire, more), 0)
        origin = iota((wire, more), 1) // EXTRA * PACK + iota((wire, more), 1) % EXTRA
        left, right = (row == origin).astype(BF16), (row == origin + EXTRA).astype(BF16)
        pack[...] = (dot(left, y2[:, :half]) + dot(right, y2[:, half:])).astype(BF16)
        columns = pl.ds(width if whole else 0, half)
        store_pack = pltpu.make_async_copy(pack, y_hbm.at[:, columns], sx.at[0])
        store_pack.start()
    if whole:

        @pl.loop(0, n2)
        def _(j):
            store(j).wait()

    if packed:
        store_pack.wait()
    if beside is not None:
        leave.wait()


def expert(x, weights, whole, packed, beside=None, fw=256, dw=512, ahead=3):
    width, hid = weights[0].shape
    wire = x.shape[0]
    rows = (wire if whole else 0) + (wire // PACK * EXTRA if packed else 0)
    n1, n2 = hid // fw, width // dw
    anywhere = pl.BlockSpec(memory_space=pl.ANY)
    args = (x,) + tuple(weights) + (() if beside is None else (beside,))
    out = (width if whole else 0) + (width // 2 if packed or beside is not None else 0)
    spare = (16, 128)
    return pl.pallas_call(
        functools.partial(expert_kernel, whole=whole, packed=packed, fw=fw, dw=dw, ahead=ahead),
        out_shape=jax.ShapeDtypeStruct((wire, out), BF16),
        in_specs=[anywhere] * len(args),
        out_specs=anywhere,
        scratch_shapes=[
            pltpu.VMEM((wire, width // 2) if packed or beside is not None else spare, BF16),
            pltpu.VMEM((rows, width), BF16),
            pltpu.VMEM((2 * n1, width, fw), BF16),
            pltpu.VMEM((n2, 2 * hid, dw), BF16),
            pltpu.VMEM((rows, 2 * hid), BF16),
            pltpu.VMEM((n2, wire, dw) if whole else (1,) + spare, BF16),
            pltpu.VMEM((wire // PACK * EXTRA, width) if packed else spare, BF16),
            pltpu.SemaphoreType.DMA((2,)),
            pltpu.SemaphoreType.DMA((2 * n1,)),
            pltpu.SemaphoreType.DMA((2, n2)),
            pltpu.SemaphoreType.DMA((n2,)),
        ],
        compiler_params=pltpu.CompilerParams(vmem_limit_bytes=60 * 2**20),
        cost_estimate=pl.CostEstimate(
            flops=8 * rows * width * hid,
            bytes_accessed=8 * width * hid + 4 * rows * width,
            transcendentals=2 * rows * hid,
        ),
        name="expert_whole" if not packed else "expert_both" if whole else "expert_packed",
    )(*args)


def unused(shape, after):
    anywhere = pl.BlockSpec(memory_space=pl.ANY)
    return pl.pallas_call(
        lambda after, out: None,
        out_shape=jax.ShapeDtypeStruct(shape, BF16),
        in_specs=[anywhere],
        out_specs=anywhere,
        name="unused",
    )(after)


def swap(x, peers):
    chunks = x.reshape(peers, x.shape[0] // peers, x.shape[1])
    return lax.all_to_all(chunks, "expert", split_axis=0, concat_axis=0, tiled=True).reshape(x.shape)


def per_device(tokens, expert_ids, gate_weights, w_in, w_out):
    peers = lax.axis_size("expert")
    cores = lax.axis_size("dp")
    turn = [(i, (i + 1) % cores) for i in range(cores)]
    other_in = lax.ppermute(w_in, "dp", turn)
    other_out = lax.ppermute(w_out, "dp", turn)
    first = lax.axis_index("dp") == 0

    def send_whole(ids, tokens):
        place, sent, pack = prep(ids, tokens, peers, apart=True)
        arrived = swap(sent, peers)
        return place, arrived, pack, unused((sent.shape[0], sent.shape[1] + pack.shape[1]), arrived)

    def send_later(ids, tokens):
        place, sent = prep(ids, tokens, peers, apart=False)
        rows, width = sent.shape[0], tokens.shape[1]
        return place, unused((rows, width), sent), unused((rows, width // 2), sent), sent

    def two_parts(routed, gates, tokens, weights):
        place, arrived, pack, _ = routed
        mixed = swap(expert(arrived, weights, whole=True, packed=False, beside=pack), peers)
        back = swap(expert(mixed, weights, whole=False, packed=True), peers)
        part = add_rows(sum_whole_kernel, place, gates, tokens, mixed, F32, "sum_whole")
        return add_rows(sum_packed_kernel, place, gates, part, back, BF16, "sum_packed")

    def one_part(routed, gates, tokens, weights):
        place, _, _, sent = routed
        back = swap(expert(swap(sent, peers), weights, whole=True, packed=True), peers)
        return combine(place, gates, tokens, back, back, 40)

    routed = lax.cond(first, send_whole, send_later, expert_ids.T, tokens)
    routed, other_in, other_out = lax.optimization_barrier((routed, other_in, other_out))
    weights = (w_in[0], other_in[0], w_out[0], other_out[0])
    return lax.cond(first, two_parts, one_part, routed, gate_weights.T, tokens, weights)


def solution(mesh):
    placed = (
        P(("dp", "expert"), None),
        P(("dp", "expert"), None),
        P(("dp", "expert"), None),
        P("expert", None, "dp"),
        P("expert", "dp", None),
    )
    return jax.shard_map(
        per_device, mesh=mesh, in_specs=placed, out_specs=P(("dp", "expert"), None), check_vma=False
    )
```

```python
import functools

import jax
import jax.numpy as jnp
from jax import lax
from jax.experimental import pallas as pl
from jax.experimental.pallas import tpu as pltpu
from jax.sharding import PartitionSpec as P

PACK = 8
EXTRA = 4
BF16 = jnp.bfloat16
F32 = jnp.float32


def iota(shape, dim):
    return lax.broadcasted_iota(jnp.int32, shape, dim)


def dot(a, b):
    return jnp.dot(a, b, preferred_element_type=F32)


def dot_t(a, b):
    return lax.dot_general(a, b, (((0,), (0,)), ((), ())), preferred_element_type=F32)


def prep_kernel(ids_ref, tok_ref, place_ref, out_ref, *pack_refs, peers):
    tokens = tok_ref.shape[0]
    width = tok_ref.shape[1]
    half = width // 2
    rows = peers * PACK
    before = (iota((tokens, tokens), 0) < iota((tokens, tokens), 1)).astype(BF16)
    experts = iota((peers, tokens), 0)
    first = experts == ids_ref[0:1, :]
    second = experts == ids_ref[1:2, :]
    first_f, second_f = first.astype(F32), second.astype(F32)
    rank0 = jnp.sum(dot(first.astype(BF16), before) * first_f, 0, keepdims=True)
    count0 = jnp.sum(first_f, 1, keepdims=True)
    rank1 = jnp.sum((dot(second.astype(BF16), before) + count0) * second_f, 0, keepdims=True)
    rank = jnp.concatenate([rank0, rank1], 0).astype(jnp.int32)
    base = ids_ref[...] * PACK + rank
    whole = jnp.where(rank < PACK, base, -rows)
    split = jnp.where(rank < PACK, -rows, base - PACK)
    place_ref[0:2, :] = whole
    place_ref[2:4, :] = split
    row = iota((rows, tokens), 0)
    pick = ((row == whole[0:1, :]) | (row == whole[1:2, :])).astype(BF16)
    left = ((row == split[0:1, :]) | (row == split[1:2, :])).astype(BF16)
    right = ((row == split[0:1, :] + EXTRA) | (row == split[1:2, :] + EXTRA)).astype(BF16)
    step = width // 7
    for c in range(0, width, step):
        out_ref[:, c : c + step] = dot(pick, tok_ref[:, c : c + step]).astype(BF16)
    step = half // 7
    for c in range(0, half, step):
        part = dot(left, tok_ref[:, c : c + step])
        part = part + dot(right, tok_ref[:, half + c : half + c + step])
        if pack_refs:
            pack_refs[0][:, c : c + step] = part.astype(BF16)
        else:
            out_ref[:, width + c : width + c + step] = part.astype(BF16)


def prep(ids, tokens, peers, apart):
    count, width = tokens.shape
    pack = (jax.ShapeDtypeStruct((peers * PACK, width // 2), BF16),) if apart else ()
    sent = width if apart else width + width // 2
    return pl.pallas_call(
        functools.partial(prep_kernel, peers=peers),
        out_shape=(
            jax.ShapeDtypeStruct((4, count), jnp.int32),
            jax.ShapeDtypeStruct((peers * PACK, sent), BF16),
        )
        + pack,
        compiler_params=pltpu.CompilerParams(vmem_limit_bytes=40 * 2**20),
        name="dispatch_rows",
    )(ids, tokens)


def gate_matrix_kernel(place_ref, gate_ref, after, out_ref):
    rows, tokens = out_ref.shape[1:]
    row = iota((rows, tokens), 0)
    out_ref[0] = gate_weights_of(row, place_ref[0:2, :], gate_ref[...])
    for side in range(2):
        out_ref[1 + side] = gate_weights_of(row, place_ref[2:4, :] + EXTRA * side, gate_ref[...])


def gate_matrices(place, gates, after):
    inside, anywhere = pl.BlockSpec(memory_space=pltpu.VMEM), pl.BlockSpec(memory_space=pl.ANY)
    return pl.pallas_call(
        gate_matrix_kernel,
        out_shape=jax.ShapeDtypeStruct((3, after.shape[0], place.shape[1]), BF16),
        in_specs=[inside, inside, anywhere],
        compiler_params=pltpu.CompilerParams(vmem_limit_bytes=32 * 2**20),
        name="gate_matrices",
    )(place, gates, after)


def combine_kernel(weight_ref, tok_ref, back_ref, pack_ref, out_ref):
    width = tok_ref.shape[1]
    half = width // 2
    step = half // 7
    for side in range(2):
        for c in range(0, half, step):
            at = side * half + c
            total = tok_ref[:, at : at + step].astype(F32)
            total = total + dot_t(weight_ref[0], back_ref[:, at : at + step])
            total = total + dot_t(weight_ref[1 + side], pack_ref[:, c : c + step])
            out_ref[:, at : at + step] = total.astype(BF16)


def combine(weight, tokens, back):
    width = tokens.shape[1]
    rows = back.shape[0]

    def block(shape, at=0):
        return pl.BlockSpec(shape, lambda i: (0, at))

    return pl.pallas_call(
        combine_kernel,
        out_shape=jax.ShapeDtypeStruct(tokens.shape, BF16),
        grid=(1,),
        in_specs=[
            pl.BlockSpec(weight.shape, lambda i: (0, 0, 0)),
            block(tokens.shape),
            block((rows, width)),
            block((rows, width // 2), 2),
        ],
        out_specs=block(tokens.shape),
        compiler_params=pltpu.CompilerParams(vmem_limit_bytes=40 * 2**20),
        name="weighted_rows",
    )(weight, tokens, back, back)


def gate_weights_of(row, place, gate):
    w = jnp.where(row == place[0:1, :], gate[0:1, :], 0.0)
    return (w + jnp.where(row == place[1:2, :], gate[1:2, :], 0.0)).astype(BF16)


def sum_whole_kernel(place_ref, gate_ref, tok_ref, back_ref, out_ref):
    tokens, width = tok_ref.shape
    row = iota((back_ref.shape[0], tokens), 0)
    whole = gate_weights_of(row, place_ref[0:2, :], gate_ref[...])
    step = width // 14
    for c in range(0, width, step):
        total = tok_ref[:, c : c + step].astype(F32) + dot_t(whole, back_ref[:, c : c + step])
        out_ref[:, c : c + step] = total.astype(BF16)


def sum_packed_kernel(place_ref, gate_ref, part_ref, pack_ref, out_ref):
    tokens, width = part_ref.shape
    half = width // 2
    row = iota((pack_ref.shape[0], tokens), 0)
    step = half // 7
    for side in range(2):
        extra = gate_weights_of(row, place_ref[2:4, :] + EXTRA * side, gate_ref[...])
        for c in range(0, half, step):
            at = side * half + c
            total = part_ref[:, at : at + step].astype(F32) + dot_t(extra, pack_ref[:, c : c + step])
            out_ref[:, at : at + step] = total.astype(BF16)


def add_rows(kernel, place, gates, base, back, out_type, name):
    count, width = base.shape
    rows = back.shape[0]

    def block(shape):
        return pl.BlockSpec(shape, lambda i: (0, 0))

    return pl.pallas_call(
        kernel,
        out_shape=jax.ShapeDtypeStruct(base.shape, out_type),
        grid=(1,),
        in_specs=[
            block(place.shape),
            block(gates.shape),
            block(base.shape),
            block((rows, min(width, back.shape[1]))),
        ],
        out_specs=block(base.shape),
        compiler_params=pltpu.CompilerParams(vmem_limit_bytes=32 * 2**20),
        cost_estimate=pl.CostEstimate(
            flops=2 * rows * base.size, bytes_accessed=12 * base.size, transcendentals=0
        ),
        name=name,
    )(place, gates, base, back)


def silu(v):
    return 0.5 * v * (1.0 + jnp.tanh(0.5 * v))


def expert_kernel(
    x_hbm, ia, ib, oa, ob, *refs, whole, packed, fw, dw, ahead
):
    y_hbm, pack, x, wi, wo, h, y, y2, sx, si, so, sy = refs[-12:]
    wire = x_hbm.shape[0]
    width = x.shape[1]
    half = width // 2
    rows = wire if whole else 0
    more = x.shape[0] - rows
    hid = ia.shape[1]
    n1, n2 = hid // fw, width // dw
    beside = refs[0] if len(refs) > 12 else None

    def part(at, size):
        return pl.ds(pl.multiple_of(at * size, size), size)

    def for_tile(t, act):
        @pl.when(t < n1)
        def _():
            act(pltpu.make_async_copy(ia.at[:, part(t, fw)], wi.at[t], si.at[t]))

        @pl.when((t >= n1) & (t < 2 * n1))
        def _():
            act(pltpu.make_async_copy(ib.at[:, part(t - n1, fw)], wi.at[t], si.at[t]))

        @pl.when((t >= 2 * n1) & (t < 2 * n1 + n2))
        def _():
            j = t - 2 * n1
            for k, src in ((0, oa), (1, ob)):
                dst = wo.at[j, pl.ds(k * hid, hid)]
                act(pltpu.make_async_copy(src.at[:, part(j, dw)], dst, so.at[k, j]))

    def start(t):
        for_tile(t, lambda copy: copy.start())

    def wait(t):
        for_tile(t, lambda copy: copy.wait())

    if packed:
        columns = pl.ds(width, half)
        fetch_pack = pltpu.make_async_copy(x_hbm.at[:, columns], pack, sx.at[0])
        fetch_pack.start()
    if whole:
        columns = pl.ds(0, width)
        fetch = pltpu.make_async_copy(x_hbm.at[:, columns], x.at[pl.ds(0, rows)], sx.at[1])
        fetch.start()

    @pl.loop(0, ahead)
    def _(t):
        start(t)

    if beside is not None:
        bring = pltpu.make_async_copy(beside, pack, sx.at[0])
        bring.start()
    if packed:
        fetch_pack.wait()
        source = iota((more, wire), 0) // EXTRA * PACK + iota((more, wire), 0) % EXTRA
        column = iota((more, wire), 1)
        x[rows:, :half] = dot((source == column).astype(BF16), pack[...]).astype(BF16)
        x[rows:, half:] = dot((source + EXTRA == column).astype(BF16), pack[...]).astype(BF16)
    if whole:
        fetch.wait()

    @pl.loop(0, 2 * n1)
    def _(t):
        start(t + ahead)
        wait(t)
        h[:, part(t, fw)] = silu(dot(x[...], wi[t])).astype(BF16)

    if beside is not None:
        bring.wait()
        leave = pltpu.make_async_copy(pack, y_hbm.at[:, pl.ds(width, half)], sx.at[0])
        leave.start()

    def store(j):
        return pltpu.make_async_copy(y.at[j], y_hbm.at[:, part(j, dw)], sy.at[j])

    @pl.loop(0, n2)
    def _(j):
        start(2 * n1 + j + ahead)
        wait(2 * n1 + j)
        if whole:
            y[j] = dot(h[:rows, :], wo[j]).astype(BF16)
            store(j).start()
        if packed:
            y2[:, part(j, dw)] = dot(h[rows:, :], wo[j]).astype(BF16)

    if packed:
        row = iota((wire, more), 0)
        origin = iota((wire, more), 1) // EXTRA * PACK + iota((wire, more), 1) % EXTRA
        left, right = (row == origin).astype(BF16), (row == origin + EXTRA).astype(BF16)
        pack[...] = (dot(left, y2[:, :half]) + dot(right, y2[:, half:])).astype(BF16)
        columns = pl.ds(width if whole else 0, half)
        store_pack = pltpu.make_async_copy(pack, y_hbm.at[:, columns], sx.at[0])
        store_pack.start()
    if whole:

        @pl.loop(0, n2)
        def _(j):
            store(j).wait()

    if packed:
        store_pack.wait()
    if beside is not None:
        leave.wait()


def expert(x, weights, whole, packed, beside=None, fw=256, dw=512, ahead=3):
    width, hid = weights[0].shape
    wire = x.shape[0]
    rows = (wire if whole else 0) + (wire // PACK * EXTRA if packed else 0)
    n1, n2 = hid // fw, width // dw
    anywhere = pl.BlockSpec(memory_space=pl.ANY)
    args = (x,) + tuple(weights) + (() if beside is None else (beside,))
    out = (width if whole else 0) + (width // 2 if packed or beside is not None else 0)
    spare = (16, 128)
    return pl.pallas_call(
        functools.partial(expert_kernel, whole=whole, packed=packed, fw=fw, dw=dw, ahead=ahead),
        out_shape=jax.ShapeDtypeStruct((wire, out), BF16),
        in_specs=[anywhere] * len(args),
        out_specs=anywhere,
        scratch_shapes=[
            pltpu.VMEM((wire, width // 2) if packed or beside is not None else spare, BF16),
            pltpu.VMEM((rows, width), BF16),
            pltpu.VMEM((2 * n1, width, fw), BF16),
            pltpu.VMEM((n2, 2 * hid, dw), BF16),
            pltpu.VMEM((rows, 2 * hid), BF16),
            pltpu.VMEM((n2, wire, dw) if whole else (1,) + spare, BF16),
            pltpu.VMEM((wire // PACK * EXTRA, width) if packed else spare, BF16),
            pltpu.SemaphoreType.DMA((2,)),
            pltpu.SemaphoreType.DMA((2 * n1,)),
            pltpu.SemaphoreType.DMA((2, n2)),
            pltpu.SemaphoreType.DMA((n2,)),
        ],
        compiler_params=pltpu.CompilerParams(vmem_limit_bytes=60 * 2**20),
        cost_estimate=pl.CostEstimate(
            flops=8 * rows * width * hid,
            bytes_accessed=8 * width * hid + 4 * rows * width,
            transcendentals=2 * rows * hid,
        ),
        name="expert_whole" if not packed else "expert_both" if whole else "expert_packed",
    )(*args)


def unused(shape, after):
    anywhere = pl.BlockSpec(memory_space=pl.ANY)
    return pl.pallas_call(
        lambda after, out: None,
        out_shape=jax.ShapeDtypeStruct(shape, BF16),
        in_specs=[anywhere],
        out_specs=anywhere,
        name="unused",
    )(after)


def swap(x, peers):
    chunks = x.reshape(peers, x.shape[0] // peers, x.shape[1])
    return lax.all_to_all(chunks, "expert", split_axis=0, concat_axis=0, tiled=True).reshape(x.shape)


def per_device(tokens, expert_ids, gate_weights, w_in, w_out):
    peers = lax.axis_size("expert")
    cores = lax.axis_size("dp")
    turn = [(i, (i + 1) % cores) for i in range(cores)]
    other_in = lax.ppermute(w_in, "dp", turn)
    other_out = lax.ppermute(w_out, "dp", turn)
    first = lax.axis_index("dp") == 0

    def send_whole(ids, tokens):
        place, sent, pack = prep(ids, tokens, peers, apart=True)
        arrived = swap(sent, peers)
        return place, arrived, pack, unused((sent.shape[0], sent.shape[1] + pack.shape[1]), arrived)

    def send_later(ids, tokens):
        place, sent = prep(ids, tokens, peers, apart=False)
        rows, width = sent.shape[0], tokens.shape[1]
        return place, unused((rows, width), sent), unused((rows, width // 2), sent), sent

    def two_parts(routed, gates, tokens, weights):
        place, arrived, pack, _ = routed
        mixed = swap(expert(arrived, weights, whole=True, packed=False, beside=pack), peers)
        back = swap(expert(mixed, weights, whole=False, packed=True), peers)
        part = add_rows(sum_whole_kernel, place, gates, tokens, mixed, BF16, "sum_whole")
        return add_rows(sum_packed_kernel, place, gates, part, back, BF16, "sum_packed")

    def one_part(routed, gates, tokens, weights):
        place, _, _, sent = routed
        outgoing = expert(swap(sent, peers), weights, whole=True, packed=True)
        back = swap(outgoing, peers)
        return combine(gate_matrices(place, gates, outgoing), tokens, back)

    routed = lax.cond(first, send_whole, send_later, expert_ids.T, tokens)
    routed, other_in, other_out = lax.optimization_barrier((routed, other_in, other_out))
    weights = (w_in[0], other_in[0], w_out[0], other_out[0])
    return lax.cond(first, two_parts, one_part, routed, gate_weights.T, tokens, weights)


def solution(mesh):
    placed = (
        P(("dp", "expert"), None),
        P(("dp", "expert"), None),
        P(("dp", "expert"), None),
        P("expert", None, "dp"),
        P("expert", "dp", None),
    )
    return jax.shard_map(
        per_device, mesh=mesh, in_specs=placed, out_specs=P(("dp", "expert"), None), check_vma=False
    )
```
